32 devices in a mesh: groups: 2 (over x), owner: 8 (over z, y), dp: 2 (over core).
Axes of the slice: x: 2, y: 2, z: 4, core: 2. Of those that a mesh axis runs over, the one named last changes fastest.
Arguments:
- activations: bfloat16 [4, 16, 28672], P(('groups', 'dp'), 'owner'), parts along dimension 0, may hold values from -6 to 6
- out_grads: bfloat16 [4, 16, 8192], P(('groups', 'dp'), 'owner'), parts along dimension 0, may hold values from -6 to 6
- lengths: int32 [4, 4], P('groups'), parts along dimension 0, may hold values from 1 to 8, 16 in all within a row
- rollout_ids: int32 [16], P('groups'), parts along dimension 0, may hold values from 0 to 7, each once
- basis_in: bfloat16 [28672, 16384], P(None, ('owner', 'dp')), may hold values from -0.03125 to 0.03125
- basis_out: bfloat16 [8192, 8192], P(None, ('owner', 'dp')), may hold values from -0.0625 to 0.0625
- eigvals: bfloat16 [8192, 16384], P(None, ('owner', 'dp')), may hold values from 0.049804688 to 5
- query_out: bfloat16 [128, 8, 8192], P(None, None, ('owner', 'dp')), may hold values from -0.0078125 to 0.0078125
- query_in: bfloat16 [128, 8, 16384], P(None, None, ('owner', 'dp')), may hold values from -0.005859375 to 0.005859375
- query_ids: int32 [64], P('groups'), parts along dimension 0, may hold values from 0 to 127
Outputs:
- influence: float32 [16, 32], P('groups'), parts along dimension 0
The draws below stay inside these ranges and needn't reach their ends.
There are 2 independent parts, one for each index of `groups`. The reference program is written for one: setup_inputs(seed, part) draws one part's arguments, and reference() takes and returns one part's arrays. A program takes and returns all parts, laid end to end along the dimension named above; an argument that names none is the same for every part. Nothing has to cross between parts.
Inputs may be any that keep to these rules, and one draw needn't show every extreme that they name: Each replica's lengths sum to 16, and its longest rollout has exactly 8 tokens. `rollout_ids`: each rollout number appears once.
All inputs are finite; a program needn't handle non-finite values.
Results may differ from the reference program's by a relative error of at most 0.005.
Values may be sent and summed in bfloat16 or wider, within the bound.
A program may use at most 256 MiB of HBM per device.

```python
import math
import jax
import jax.numpy as jnp
import numpy as np
from jax import lax

D_IN = 28672
D_OUT = 8192
K_A = 16384
K_S = 8192
RANK = 8
QBANK = 128
NQ = 32
RO_REP = 4
REP_TOK = 16
ROLLOUTS = 8
N_DP = 2


def with_ends(array, key, least, largest):
    dims = array.shape
    place = [jax.random.randint(jax.random.fold_in(key, axis), (), 0, dims[axis]) for axis in range(len(dims))]
    array = array.at[tuple(place)].set(least)
    longest = dims.index(max(dims))
    place[longest] = (place[longest] + 1) % dims[longest]
    return array.at[tuple(place)].set(largest)


def levels(key, extent, cuts, smallest, high):
    gain = 1.0
    for axis_at, parts in cuts:
        steps = jax.random.uniform(jax.random.fold_in(jax.random.fold_in(key, 6), axis_at), (parts,), jnp.float32, smallest / len(cuts), high / len(cuts))
        gain = gain * jnp.repeat(jnp.exp(steps), extent[axis_at] // parts).reshape((-1,) + (1,) * (len(extent) - 1 - axis_at))
    return gain


def length_profile(count, total, most, lean):
    loads = [(1 << 20) // math.isqrt(standing ** lean) + 1 for standing in range(2, count + 1)]
    spare, holding = total - most - (count - 1), [1] * (count - 1)
    while spare > 0:
        movable = [i for i in range(count - 1) if holding[i] < most]
        whole, budget = sum([loads[i] for i in movable]), spare
        for i in movable:
            addition = min(most - holding[i], max(1, budget * loads[i] // whole), spare)
            holding[i] = holding[i] + addition
            spare = spare - addition
    return np.array([most] + holding)


def uneven(own_key, count, total, bound, lean):
    if count == 2:
        one = jax.random.randint(own_key, (), max(1, total - bound), min(bound, total - 1) + 1)
        return jnp.stack([one, total - one])
    sizes = jnp.asarray(length_profile(count, total, bound, lean), jnp.int32)
    pairs = (count - 1) // 2
    donor, receiver = sizes[1:1 + 2 * pairs:2], sizes[2:2 + 2 * pairs:2]
    room = jnp.minimum(donor - 1, bound - receiver)
    moved = jax.random.randint(jax.random.fold_in(own_key, 1), (pairs,), 0, 1 << 20) % (room + 1)
    sizes = sizes.at[1:1 + 2 * pairs:2].set(donor - moved).at[2:2 + 2 * pairs:2].set(receiver + moved)
    return sizes[jax.random.permutation(jax.random.fold_in(own_key, 2), count)]


def noise(own_key, extent, scale, most, cuts=(), kind=jnp.bfloat16):
    factor_of = levels(own_key, extent, cuts, -0.22, 0.18) if cuts else 1.0
    array = jax.random.normal(own_key, extent, jnp.float32) * scale * factor_of
    return jnp.minimum(jnp.maximum(array, -most), most).astype(kind)


def setup_inputs(seed: int = 0, part: int = 0) -> dict:
    key_of = jax.random.split(jax.random.key(seed), 11)
    own_keys = jax.random.split(jax.random.fold_in(key_of[10], part), 11)
    return {
        "activations": noise(own_keys[0], (N_DP, REP_TOK, D_IN), 1.0, 6.0, ((0, 2), (1, 8))),
        "out_grads": noise(own_keys[1], (N_DP, REP_TOK, D_OUT), 1.0, 6.0, ((0, 2), (1, 8))),
        "lengths": jax.vmap(lambda own: uneven(own, RO_REP, REP_TOK, REP_TOK // 2, 2))(jax.random.split(own_keys[2], N_DP)).reshape((N_DP, RO_REP)).astype(jnp.int32),
        "rollout_ids": jax.random.permutation(own_keys[3], ROLLOUTS).astype(jnp.int32),
        "basis_in": noise(key_of[4], (D_IN, K_A), D_IN ** -0.5, 0.03125, ((1, 16),)),
        "basis_out": noise(key_of[5], (D_OUT, K_S), D_OUT ** -0.5, 0.0625, ((1, 16),)),
        "eigvals": jnp.clip(jnp.exp(math.log(5.0) - 4.609084 * jax.random.uniform(key_of[6], (K_S, K_A), jnp.float32) ** levels(key_of[6], (K_S, K_A), ((1, 16),), -0.2, 0.2)), 0.049804688, 5.0).astype(jnp.bfloat16),
        "query_out": noise(key_of[7], (QBANK, RANK, K_S), (K_S * 64) ** -0.5, 0.0078125, ((2, 16),)),
        "query_in": noise(key_of[8], (QBANK, RANK, K_A), (K_A * 64) ** -0.5, 0.005859375, ((2, 16),)),
        "query_ids": with_ends(jax.random.randint(own_keys[9], (NQ,), 0, QBANK), jax.random.fold_in(own_keys[9], 1), 0, QBANK - 1).astype(jnp.int32),
    }


DAMPING = 0.1


def membership(lengths, slots):
    ends = jnp.cumsum(lengths, axis=1)
    starts = ends - lengths
    position = jnp.arange(slots, dtype=jnp.int32)[None, :, None]
    inside = (position >= starts[:, None, :]) & (position < ends[:, None, :])
    return inside.astype(jnp.bfloat16)


def reference(activations, out_grads, lengths, rollout_ids, basis_in, basis_out, eigvals, query_out, query_in, query_ids):
    rot_in = jnp.dot(activations.reshape(-1, D_IN), basis_in, preferred_element_type=jnp.float32).astype(jnp.bfloat16)
    rot_in = rot_in.reshape(N_DP, REP_TOK, K_A)
    rot_out = jnp.dot(out_grads.reshape(-1, D_OUT), basis_out, preferred_element_type=jnp.float32).astype(jnp.bfloat16)
    rot_out = rot_out.reshape(N_DP, REP_TOK, K_S)
    member = membership(lengths, REP_TOK)
    sel_out = query_out[query_ids].reshape(NQ * RANK, K_S)
    sel_in = query_in[query_ids].reshape(NQ * RANK, K_A).astype(jnp.float32)
    inv_eig = 1.0 / (eigvals.astype(jnp.float32) + DAMPING)
    gathered = []
    for replica in range(N_DP):
        def per_rollout(mask_col, replica=replica):
            masked = rot_in[replica] * mask_col[:, None]
            outer_sum = lax.dot_general(rot_out[replica], masked, (((0,), (0,)), ((), ())), preferred_element_type=jnp.float32)
            scaled = (outer_sum * inv_eig).astype(jnp.bfloat16)
            projected = jnp.dot(sel_out, scaled, preferred_element_type=jnp.float32)
            return jnp.sum((projected * sel_in).reshape(NQ, RANK, K_A), axis=(1, 2))
        gathered.append(lax.map(per_rollout, member[replica].T))
    scores = jnp.stack(gathered)
    placing = (rollout_ids.reshape(N_DP, RO_REP)[:, :, None] == jnp.arange(ROLLOUTS, dtype=jnp.int32)[None, None, :]).astype(jnp.float32)
    return jnp.einsum('dep,deq->pq', placing, scores)
```

```python
import functools

import jax
import jax.numpy as jnp
from jax import lax
from jax.experimental import pallas as pl
from jax.experimental.pallas import tpu as pltpu
from jax.sharding import PartitionSpec as P

DAMPING = 0.1
BOTH = ("owner", "dp")


def score_kernel(rollouts, k_tile, out_ref_t, sel_out_ref, eig_ref, masked_ref, sel_in_ref, acc_ref):
    @pl.when(pl.program_id(0) == 0)
    def _():
        acc_ref[...] = jnp.zeros_like(acc_ref)

    rows, columns = eig_ref.shape
    wide = sel_in_ref.shape[1]
    damped = eig_ref[...].astype(jnp.float32) + DAMPING
    rough = pl.reciprocal(damped, approx=True)
    inv = rough * (2.0 - damped * rough)
    tokens_t = out_ref_t[...]
    sel_out = sel_out_ref[...].astype(jnp.float32)
    for e in range(rollouts):
        turned = jnp.zeros((rows, wide), jnp.float32)
        for at in range(0, columns, k_tile):
            outer = jnp.dot(
                tokens_t, masked_ref[e, :, at : at + k_tile], preferred_element_type=jnp.float32
            )
            scaled = (outer * inv[:, at : at + k_tile]).astype(jnp.bfloat16)
            turned += jnp.dot(
                scaled, sel_in_ref[at : at + k_tile, :], preferred_element_type=jnp.float32
            )
        acc_ref[e] += jnp.sum((turned * sel_out).reshape(rows // 8, 8, wide), axis=0)


def plane_scores(rot_out_t, sel_out_t, eigvals, masked_in, sel_in_t):
    total, columns = eigvals.shape
    rollouts, tokens, _ = masked_in.shape
    wide = sel_in_t.shape[1]
    rows = min(512, total)
    k_tile = min(256, columns)
    return pl.pallas_call(
        functools.partial(score_kernel, rollouts, k_tile),
        grid=(total // rows,),
        in_specs=[
            pl.BlockSpec((rows, tokens), lambda i: (i, 0)),
            pl.BlockSpec((rows, wide), lambda i: (i, 0)),
            pl.BlockSpec((rows, columns), lambda i: (i, 0)),
            pl.BlockSpec((rollouts, tokens, columns), lambda i: (0, 0, 0)),
            pl.BlockSpec((columns, wide), lambda i: (0, 0)),
        ],
        out_specs=pl.BlockSpec((rollouts, 8, wide), lambda i: (0, 0, 0)),
        out_shape=jax.ShapeDtypeStruct((rollouts, 8, wide), jnp.float32),
        compiler_params=pltpu.CompilerParams(vmem_limit_bytes=48 * 1024 * 1024),
        cost_estimate=pl.CostEstimate(
            flops=2 * rollouts * total * columns * (wide + 256),
            bytes_accessed=2 * total * (columns + wide),
            transcendentals=total * columns,
        ),
    )(rot_out_t, sel_out_t, eigvals, masked_in, sel_in_t)


def on_device(
    activations,
    out_grads,
    lengths,
    rollout_ids,
    basis_in,
    basis_out,
    eigvals,
    query_out,
    query_in,
    query_ids,
):
    queries = query_ids.shape[0]
    bank, rank, _ = query_out.shape
    slots = activations.shape[1]
    owners = lax.axis_size("owner")
    replicas = lax.axis_size("dp")
    per_replica = lengths.shape[1]
    rollouts = rollout_ids.shape[0]
    tokens = owners * replicas * slots
    picker = (query_ids[:, None] == jnp.arange(bank, dtype=jnp.int32)[None, :]).astype(jnp.bfloat16)

    grads = lax.all_gather(out_grads[0], BOTH, axis=0, tiled=True)
    acts = lax.all_gather(activations[0], BOTH, axis=0, tiled=True)
    sel_out_t = jnp.einsum(
        "qb,brj->jqr", picker, query_out, preferred_element_type=jnp.float32
    ).astype(jnp.bfloat16)
    sel_out_t = lax.all_gather(sel_out_t.reshape(-1, queries * rank), BOTH, axis=0, tiled=True)
    sel_in_t = jnp.einsum(
        "qb,brk->kqr", picker, query_in, preferred_element_type=jnp.float32
    ).astype(jnp.bfloat16)
    sel_in_t = sel_in_t.reshape(-1, queries * rank)

    block_out = jnp.dot(grads, basis_out, preferred_element_type=jnp.float32).astype(jnp.bfloat16)
    rot_out_t = lax.all_gather(block_out.T, BOTH, axis=0, tiled=True)
    rot_in = jnp.dot(acts, basis_in, preferred_element_type=jnp.float32).astype(jnp.bfloat16)

    token = jnp.arange(tokens, dtype=jnp.int32)
    place = (token // (replicas * slots)) * slots + token % slots
    replica = (token // slots) % replicas
    ends = jnp.cumsum(lengths, axis=1)
    starts = ends - lengths
    member = (
        (jnp.arange(replicas, dtype=jnp.int32)[:, None, None] == replica[None, None, :])
        & (place[None, None, :] >= starts[:, :, None])
        & (place[None, None, :] < ends[:, :, None])
    ).reshape(rollouts, tokens)
    masked_in = jnp.where(member[:, :, None], rot_in[None], jnp.zeros((), rot_in.dtype))

    acc = plane_scores(rot_out_t, sel_out_t, eigvals, masked_in, sel_in_t)
    scores = jnp.sum(acc.reshape(rollouts, 8, queries, rank), axis=(1, 3))
    scores = lax.psum(scores, BOTH)
    placing = (rollout_ids[:, None] == jnp.arange(rollouts, dtype=jnp.int32)[None, :]).astype(
        jnp.float32
    )
    return jnp.sum(placing[:, :, None] * scores[:, None, :], axis=0)


def solution(mesh):
    return jax.shard_map(
        on_device,
        mesh=mesh,
        in_specs=(
            P(("groups", "dp"), "owner", None),
            P(("groups", "dp"), "owner", None),
            P("groups", None),
            P("groups"),
            P(None, BOTH),
            P(None, BOTH),
            P(None, BOTH),
            P(None, None, BOTH),
            P(None, None, BOTH),
            P("groups"),
        ),
        out_specs=P("groups", None),
        check_vma=False,
    )
```

```python
import functools

import jax
import jax.numpy as jnp
from jax import lax
from jax.experimental import pallas as pl
from jax.experimental.pallas import tpu as pltpu
from jax.sharding import PartitionSpec as P

DAMPING = 0.1
BOTH = ("owner", "dp")


def gather_kernel(lines, along, block_ref, all_ref, send_sem, recv_sem, own_sem):
    owner, core = lax.axis_index("owner"), lax.axis_index("dp")
    line, place = owner // along, owner % along
    cores = lax.axis_size("dp")

    def index(a, b, c):
        return (a * along + b) * cores + c

    line_peers = [lax.rem(line + s, lines) for s in range(1, lines)]
    row_peers = [lax.rem(place + s, along) for s in range(1, along)]
    core_peers = [lax.rem(core + s, cores) for s in range(1, cores)]
    peers = [(a, place, core) for a in line_peers]
    peers += [(line, b, core) for b in row_peers]
    peers += [(line, place, c) for c in core_peers]

    def device(a, b, c):
        return {"owner": a * along + b, "dp": c}

    barrier = pltpu.get_barrier_semaphore()
    for peer in peers:
        pl.semaphore_signal(
            barrier, inc=1, device_id=device(*peer), device_id_type=pl.DeviceIdType.MESH
        )
    pl.semaphore_wait(barrier, len(peers))

    sent = []

    def push(source, slot, peer):
        copy = pltpu.make_async_remote_copy(
            src_ref=source,
            dst_ref=all_ref.at[slot],
            send_sem=send_sem.at[len(sent)],
            recv_sem=recv_sem.at[slot],
            device_id=device(*peer),
            device_id_type=pl.DeviceIdType.MESH,
        )
        copy.start()
        sent.append(copy)

    def arrived(slot):
        pltpu.make_async_copy(block_ref, all_ref.at[slot], recv_sem.at[slot]).wait()

    mine = index(line, place, core)
    for peer in peers:
        push(block_ref, mine, peer)
    own = pltpu.make_async_copy(block_ref, all_ref.at[mine], own_sem)
    own.start()
    for a in line_peers:
        slot = index(a, place, core)
        arrived(slot)
        for b in row_peers:
            push(all_ref.at[slot], slot, (line, b, core))
        for c in core_peers:
            push(all_ref.at[slot], slot, (line, place, c))
    for a in [line] + line_peers:
        for b in row_peers:
            slot = index(a, b, core)
            arrived(slot)
            for c in core_peers:
                push(all_ref.at[slot], slot, (line, place, c))
    for c in core_peers:
        for a in [line] + line_peers:
            for b in [place] + row_peers:
                arrived(index(a, b, c))
    own.wait()
    for copy in sent:
        copy.wait_send()


def gather_blocks(block, collective_id):
    owners, cores = lax.axis_size("owner"), lax.axis_size("dp")
    along = 2 if owners < 16 else 8
    lines = owners // along
    copies = lines + along + cores - 3
    copies += (lines - 1) * (along + cores - 2) + lines * (along - 1) * (cores - 1)
    return pl.pallas_call(
        functools.partial(gather_kernel, lines, along),
        in_specs=[pl.BlockSpec(memory_space=pl.ANY)],
        out_specs=pl.BlockSpec(memory_space=pl.ANY),
        out_shape=jax.ShapeDtypeStruct((owners * cores,) + block.shape, block.dtype),
        scratch_shapes=[
            pltpu.SemaphoreType.DMA((copies,)),
            pltpu.SemaphoreType.DMA((owners * cores,)),
            pltpu.SemaphoreType.DMA,
        ],
        compiler_params=pltpu.CompilerParams(
            collective_id=collective_id, has_side_effects=True
        ),
        cost_estimate=pl.CostEstimate(
            flops=0, bytes_accessed=2 * owners * cores * block.size * 2, transcendentals=0
        ),
    )(block)


def score_kernel(rollouts, k_tile, out_ref_t, sel_out_ref, eig_ref, masked_ref, sel_in_ref, acc_ref):
    @pl.when(pl.program_id(0) == 0)
    def _():
        acc_ref[...] = jnp.zeros_like(acc_ref)

    rows, columns = eig_ref.shape
    wide = sel_in_ref.shape[1]
    damped = eig_ref[...].astype(jnp.float32) + DAMPING
    rough = pl.reciprocal(damped, approx=True)
    inv = rough * (2.0 - damped * rough)
    tokens_t = out_ref_t[...]
    sel_out = sel_out_ref[...].astype(jnp.float32)
    for e in range(rollouts):
        turned = jnp.zeros((rows, wide), jnp.float32)
        for at in range(0, columns, k_tile):
            outer = jnp.dot(
                tokens_t, masked_ref[e, :, at : at + k_tile], preferred_element_type=jnp.float32
            )
            scaled = (outer * inv[:, at : at + k_tile]).astype(jnp.bfloat16)
            turned += jnp.dot(
                scaled, sel_in_ref[at : at + k_tile, :], preferred_element_type=jnp.float32
            )
        acc_ref[e] += jnp.sum((turned * sel_out).reshape(rows // 8, 8, wide), axis=0)


def plane_scores(rot_out_t, sel_out_t, eigvals, masked_in, sel_in_t):
    total, columns = eigvals.shape
    rollouts, tokens, _ = masked_in.shape
    wide = sel_in_t.shape[1]
    rows = min(512, total)
    k_tile = min(256, columns)
    return pl.pallas_call(
        functools.partial(score_kernel, rollouts, k_tile),
        grid=(total // rows,),
        in_specs=[
            pl.BlockSpec((rows, tokens), lambda i: (i, 0)),
            pl.BlockSpec((rows, wide), lambda i: (i, 0)),
            pl.BlockSpec((rows, columns), lambda i: (i, 0)),
            pl.BlockSpec((rollouts, tokens, columns), lambda i: (0, 0, 0)),
            pl.BlockSpec((columns, wide), lambda i: (0, 0)),
        ],
        out_specs=pl.BlockSpec((rollouts, 8, wide), lambda i: (0, 0, 0)),
        out_shape=jax.ShapeDtypeStruct((rollouts, 8, wide), jnp.float32),
        compiler_params=pltpu.CompilerParams(vmem_limit_bytes=48 * 1024 * 1024),
        cost_estimate=pl.CostEstimate(
            flops=2 * rollouts * total * columns * (wide + 256),
            bytes_accessed=2 * total * (columns + wide),
            transcendentals=total * columns,
        ),
    )(rot_out_t, sel_out_t, eigvals, masked_in, sel_in_t)


def on_device(
    activations,
    out_grads,
    lengths,
    rollout_ids,
    basis_in,
    basis_out,
    eigvals,
    query_out,
    query_in,
    query_ids,
):
    queries = query_ids.shape[0]
    bank, rank, _ = query_out.shape
    slots = activations.shape[1]
    owners = lax.axis_size("owner")
    replicas = lax.axis_size("dp")
    per_replica = lengths.shape[1]
    rollouts = rollout_ids.shape[0]
    tokens = owners * replicas * slots
    picker = (query_ids[:, None] == jnp.arange(bank, dtype=jnp.int32)[None, :]).astype(jnp.bfloat16)

    wide_in, wide_out = activations.shape[2], out_grads.shape[2]
    both = jnp.concatenate(
        [activations.reshape(-1, 128), out_grads.reshape(-1, 128)], axis=0
    )
    sel_out_t = jnp.einsum(
        "qb,brj->jqr", picker, query_out, preferred_element_type=jnp.float32
    ).astype(jnp.bfloat16)
    sel_out_t = lax.all_gather(sel_out_t.reshape(-1, queries * rank), BOTH, axis=0, tiled=True)
    sel_in_t = jnp.einsum(
        "qb,brk->kqr", picker, query_in, preferred_element_type=jnp.float32
    ).astype(jnp.bfloat16)
    sel_in_t = sel_in_t.reshape(-1, queries * rank)

    gathered = gather_blocks(both, 0)
    split = slots * wide_in // 128
    acts = gathered[:, :split].reshape(tokens, wide_in)
    grads = gathered[:, split:].reshape(tokens, wide_out)
    block_out = jnp.dot(grads, basis_out, preferred_element_type=jnp.float32).astype(jnp.bfloat16)
    rot_out_t = gather_blocks(block_out, 1).transpose(0, 2, 1).reshape(-1, tokens)
    rot_in = jnp.dot(acts, basis_in, preferred_element_type=jnp.float32).astype(jnp.bfloat16)

    token = jnp.arange(tokens, dtype=jnp.int32)
    place = (token // (replicas * slots)) * slots + token % slots
    replica = (token // slots) % replicas
    ends = jnp.cumsum(lengths, axis=1)
    starts = ends - lengths
    member = (
        (jnp.arange(replicas, dtype=jnp.int32)[:, None, None] == replica[None, None, :])
        & (place[None, None, :] >= starts[:, :, None])
        & (place[None, None, :] < ends[:, :, None])
    ).reshape(rollouts, tokens)
    masked_in = jnp.where(member[:, :, None], rot_in[None], jnp.zeros((), rot_in.dtype))

    acc = plane_scores(rot_out_t, sel_out_t, eigvals, masked_in, sel_in_t)
    scores = jnp.sum(acc.reshape(rollouts, 8, queries, rank), axis=(1, 3))
    shares = gather_blocks(jnp.pad(scores, ((0, 0), (0, -queries % 128))), 2)
    scores = jnp.sum(shares, axis=0)[:, :queries]
    placing = (rollout_ids[:, None] == jnp.arange(rollouts, dtype=jnp.int32)[None, :]).astype(
        jnp.float32
    )
    return jnp.sum(placing[:, :, None] * scores[:, None, :], axis=0)


def solution(mesh):
    return jax.shard_map(
        on_device,
        mesh=mesh,
        in_specs=(
            P(("groups", "dp"), "owner", None),
            P(("groups", "dp"), "owner", None),
            P("groups", None),
            P("groups"),
            P(None, BOTH),
            P(None, BOTH),
            P(None, BOTH),
            P(None, None, BOTH),
            P(None, None, BOTH),
            P("groups"),
        ),
        out_specs=P("groups", None),
        check_vma=False,
    )
```

```python
import functools

import jax
import jax.numpy as jnp
from jax import lax
from jax.experimental import pallas as pl
from jax.experimental.pallas import tpu as pltpu
from jax.sharding import PartitionSpec as P

DAMPING = 0.1
BOTH = ("owner", "dp")


def gather_kernel(lines, along, arrays, *refs):
    blocks, alls = refs[:arrays], refs[arrays : 2 * arrays]
    send_sem, recv_sem, own_sem = refs[2 * arrays :]
    owner, core = lax.axis_index("owner"), lax.axis_index("dp")
    line, place = owner // along, owner % along
    cores = lax.axis_size("dp")

    def index(a, b, c):
        return (a * along + b) * cores + c

    line_peers = [lax.rem(line + s, lines) for s in range(1, lines)]
    row_peers = [lax.rem(place + s, along) for s in range(1, along)]
    core_peers = [lax.rem(core + s, cores) for s in range(1, cores)]
    peers = [(a, place, core) for a in line_peers]
    peers += [(line, b, core) for b in row_peers]
    peers += [(line, place, c) for c in core_peers]

    def device(a, b, c):
        return {"owner": a * along + b, "dp": c}

    barrier = pltpu.get_barrier_semaphore()
    for peer in peers:
        pl.semaphore_signal(
            barrier, inc=1, device_id=device(*peer), device_id_type=pl.DeviceIdType.MESH
        )
    pl.semaphore_wait(barrier, len(peers))

    sent = []

    def push(sources, slot, peer):
        for n in range(arrays):
            copy = pltpu.make_async_remote_copy(
                src_ref=sources[n],
                dst_ref=alls[n].at[slot],
                send_sem=send_sem.at[len(sent)],
                recv_sem=recv_sem.at[n, slot],
                device_id=device(*peer),
                device_id_type=pl.DeviceIdType.MESH,
            )
            copy.start()
            sent.append(copy)

    def arrived(slot):
        for n in range(arrays):
            pltpu.make_async_copy(blocks[n], alls[n].at[slot], recv_sem.at[n, slot]).wait()

    def held(slot):
        return [whole.at[slot] for whole in alls]

    mine = index(line, place, core)
    for peer in peers:
        push(blocks, mine, peer)
    own = [
        pltpu.make_async_copy(blocks[n], alls[n].at[mine], own_sem.at[n]) for n in range(arrays)
    ]
    for copy in own:
        copy.start()
    for a in line_peers:
        slot = index(a, place, core)
        arrived(slot)
        for b in row_peers:
            push(held(slot), slot, (line, b, core))
        for c in core_peers:
            push(held(slot), slot, (line, place, c))
    for a in [line] + line_peers:
        for b in row_peers:
            slot = index(a, b, core)
            arrived(slot)
            for c in core_peers:
                push(held(slot), slot, (line, place, c))
    for c in core_peers:
        for a in [line] + line_peers:
            for b in [place] + row_peers:
                arrived(index(a, b, c))
    for copy in own:
        copy.wait()
    for copy in sent:
        copy.wait_send()


def gather_blocks(blocks, collective_id):
    owners, cores = lax.axis_size("owner"), lax.axis_size("dp")
    along = 2 if owners < 16 else 8
    lines = owners // along
    arrays = len(blocks)
    copies = lines + along + cores - 3
    copies += (lines - 1) * (along + cores - 2) + lines * (along - 1) * (cores - 1)
    return pl.pallas_call(
        functools.partial(gather_kernel, lines, along, arrays),
        in_specs=[pl.BlockSpec(memory_space=pl.ANY)] * arrays,
        out_specs=[pl.BlockSpec(memory_space=pl.ANY)] * arrays,
        out_shape=[
            jax.ShapeDtypeStruct((owners * cores,) + block.shape, block.dtype) for block in blocks
        ],
        scratch_shapes=[
            pltpu.SemaphoreType.DMA((arrays * copies,)),
            pltpu.SemaphoreType.DMA((arrays, owners * cores)),
            pltpu.SemaphoreType.DMA((arrays,)),
        ],
        compiler_params=pltpu.CompilerParams(
            collective_id=collective_id, has_side_effects=True
        ),
        cost_estimate=pl.CostEstimate(
            flops=0,
            bytes_accessed=4 * owners * cores * sum(block.size for block in blocks),
            transcendentals=0,
        ),
    )(*blocks)


def exchange_blocks(block):
    owners, cores = lax.axis_size("owner"), lax.axis_size("dp")
    count = owners * cores
    place = jnp.arange(count, dtype=jnp.int32)
    if count > 32:
        return lax.all_gather(block, BOTH, axis=0), place
    quad = 4
    far = count // quad
    pieces = [block]
    for s in range(1, quad):
        pairs = [(i, i // quad * quad + (i + s) % quad) for i in range(count)]
        pieces.append(lax.ppermute(block, BOTH, pairs))
    near = jnp.stack(pieces)
    groups = [near]
    for s in range(1, far):
        pairs = [(i, (i + quad * s) % count) for i in range(count)]
        groups.append(lax.ppermute(near, BOTH, pairs))
    me = lax.axis_index("owner") * cores + lax.axis_index("dp")
    order = (me // quad - place // quad + far) % far * quad + (me - place + count) % quad
    return jnp.concatenate(groups, axis=0), order


def score_kernel(rollouts, per, order_ref, *refs):
    out_refs = refs[:per]
    sel_out_ref, eig_ref, masked_ref, sel_in_ref, acc_ref = refs[per:]

    @pl.when(pl.program_id(0) == 0)
    def _():
        acc_ref[...] = jnp.zeros_like(acc_ref)

    rows = eig_ref.shape[0]
    wide = sel_in_ref.shape[1]
    damped = eig_ref[...].astype(jnp.float32) + DAMPING
    rough = pl.reciprocal(damped, approx=True)
    inv = rough * (2.0 - damped * rough)
    tokens_t = jnp.concatenate([ref[0].T for ref in out_refs], axis=0)
    sel_out = sel_out_ref[...].astype(jnp.float32)
    for e in range(rollouts):
        outer = jnp.dot(tokens_t, masked_ref[e], preferred_element_type=jnp.float32)
        scaled = (outer * inv).astype(jnp.bfloat16)
        turned = jnp.dot(scaled, sel_in_ref[...], preferred_element_type=jnp.float32)
        acc_ref[e] += jnp.sum((turned * sel_out).reshape(rows // 8, 8, wide), axis=0)


def plane_scores(order, rot_out, sel_out_t, eigvals, masked_in, sel_in_t):
    total, columns = eigvals.shape
    rollouts, tokens, _ = masked_in.shape
    wide = sel_in_t.shape[1]
    block = rot_out.shape[2]
    per = max(1, 1024 // block)
    rows = per * block

    def rotated(n):
        return pl.BlockSpec((1, tokens, block), lambda i, order: (order[i * per + n], 0, 0))

    return pl.pallas_call(
        functools.partial(score_kernel, rollouts, per),
        grid_spec=pltpu.PrefetchScalarGridSpec(
            num_scalar_prefetch=1,
            grid=(total // rows,),
            in_specs=[rotated(n) for n in range(per)]
            + [
                pl.BlockSpec((rows, wide), lambda i, order: (i, 0)),
                pl.BlockSpec((rows, columns), lambda i, order: (i, 0)),
                pl.BlockSpec((rollouts, tokens, columns), lambda i, order: (0, 0, 0)),
                pl.BlockSpec((columns, wide), lambda i, order: (0, 0)),
            ],
            out_specs=pl.BlockSpec((rollouts, 8, wide), lambda i, order: (0, 0, 0)),
        ),
        out_shape=jax.ShapeDtypeStruct((rollouts, 8, wide), jnp.float32),
        compiler_params=pltpu.CompilerParams(vmem_limit_bytes=56 * 1024 * 1024),
        cost_estimate=pl.CostEstimate(
            flops=2 * rollouts * total * columns * (wide + 256),
            bytes_accessed=2 * total * (columns + wide),
            transcendentals=total * columns,
        ),
    )(order, *[rot_out] * per, sel_out_t, eigvals, masked_in, sel_in_t)


def on_device(
    activations,
    out_grads,
    lengths,
    rollout_ids,
    basis_in,
    basis_out,
    eigvals,
    query_out,
    query_in,
    query_ids,
):
    queries = query_ids.shape[0]
    bank, rank, _ = query_out.shape
    slots = activations.shape[1]
    owners = lax.axis_size("owner")
    replicas = lax.axis_size("dp")
    per_replica = lengths.shape[1]
    rollouts = rollout_ids.shape[0]
    tokens = owners * replicas * slots
    picker = (query_ids[:, None] == jnp.arange(bank, dtype=jnp.int32)[None, :]).astype(jnp.bfloat16)

    wide_in, wide_out = activations.shape[2], out_grads.shape[2]
    sel_out_t = jnp.einsum(
        "qb,brj->jqr", picker, query_out, preferred_element_type=jnp.float32
    ).astype(jnp.bfloat16)
    sel_out_t = lax.all_gather(sel_out_t.reshape(-1, queries * rank), BOTH, axis=0, tiled=True)
    sel_in_t = jnp.einsum(
        "qb,brk->kqr", picker, query_in, preferred_element_type=jnp.float32
    ).astype(jnp.bfloat16)
    sel_in_t = sel_in_t.reshape(-1, queries * rank)

    acts, grads = gather_blocks([activations.reshape(-1, 128), out_grads.reshape(-1, 128)], 0)
    acts = acts.reshape(tokens, wide_in)
    grads = grads.reshape(tokens, wide_out)
    block_out = jnp.dot(grads, basis_out, preferred_element_type=jnp.float32).astype(jnp.bfloat16)
    rot_out, order = exchange_blocks(block_out)
    rot_in = jnp.dot(acts, basis_in, preferred_element_type=jnp.float32).astype(jnp.bfloat16)

    token = jnp.arange(tokens, dtype=jnp.int32)
    place = (token // (replicas * slots)) * slots + token % slots
    replica = (token // slots) % replicas
    ends = jnp.cumsum(lengths, axis=1)
    starts = ends - lengths
    member = (
        (jnp.arange(replicas, dtype=jnp.int32)[:, None, None] == replica[None, None, :])
        & (place[None, None, :] >= starts[:, :, None])
        & (place[None, None, :] < ends[:, :, None])
    ).reshape(rollouts, tokens)
    masked_in = jnp.where(member[:, :, None], rot_in[None], jnp.zeros((), rot_in.dtype))

    acc = plane_scores(order, rot_out, sel_out_t, eigvals, masked_in, sel_in_t)
    scores = jnp.sum(acc.reshape(rollouts, 8, queries, rank), axis=(1, 3))
    shares = gather_blocks([jnp.pad(scores, ((0, 0), (0, -queries % 128)))], 1)[0]
    scores = jnp.sum(shares, axis=0)[:, :queries]
    placing = (rollout_ids[:, None] == jnp.arange(rollouts, dtype=jnp.int32)[None, :]).astype(
        jnp.float32
    )
    return jnp.sum(placing[:, :, None] * scores[:, None, :], axis=0)


def solution(mesh):
    return jax.shard_map(
        on_device,
        mesh=mesh,
        in_specs=(
            P(("groups", "dp"), "owner", None),
            P(("groups", "dp"), "owner", None),
            P("groups", None),
            P("groups"),
            P(None, BOTH),
            P(None, BOTH),
            P(None, BOTH),
            P(None, None, BOTH),
            P(None, None, BOTH),
            P("groups"),
        ),
        out_specs=P("groups", None),
        check_vma=False,
    )
```

```python
import functools

import jax
import jax.numpy as jnp
from jax import lax
from jax.experimental import pallas as pl
from jax.experimental.pallas import tpu as pltpu
from jax.sharding import PartitionSpec as P

DAMPING = 0.1
BOTH = ("owner", "dp")


def gather_kernel(lines, along, arrays, *refs):
    blocks, alls = refs[:arrays], refs[arrays : 2 * arrays]
    send_sem, recv_sem, own_sem = refs[2 * arrays :]
    owner, core = lax.axis_index("owner"), lax.axis_index("dp")
    line, place = owner // along, owner % along
    cores = lax.axis_size("dp")

    def index(a, b, c):
        return (a * along + b) * cores + c

    line_peers = [lax.rem(line + s, lines) for s in range(1, lines)]
    row_peers = [lax.rem(place + s, along) for s in range(1, along)]
    core_peers = [lax.rem(core + s, cores) for s in range(1, cores)]
    peers = [(a, place, core) for a in line_peers]
    peers += [(line, b, core) for b in row_peers]
    peers += [(line, place, c) for c in core_peers]

    def device(a, b, c):
        return {"owner": a * along + b, "dp": c}

    barrier = pltpu.get_barrier_semaphore()
    for peer in peers:
        pl.semaphore_signal(
            barrier, inc=1, device_id=device(*peer), device_id_type=pl.DeviceIdType.MESH
        )
    pl.semaphore_wait(barrier, len(peers))

    sent = []

    def push(sources, slot, peer):
        for n in range(arrays):
            copy = pltpu.make_async_remote_copy(
                src_ref=sources[n],
                dst_ref=alls[n].at[slot],
                send_sem=send_sem.at[len(sent)],
                recv_sem=recv_sem.at[n, slot],
                device_id=device(*peer),
                device_id_type=pl.DeviceIdType.MESH,
            )
            copy.start()
            sent.append(copy)

    def arrived(slot):
        for n in range(arrays):
            pltpu.make_async_copy(blocks[n], alls[n].at[slot], recv_sem.at[n, slot]).wait()

    def held(slot):
        return [whole.at[slot] for whole in alls]

    mine = index(line, place, core)
    for peer in peers:
        push(blocks, mine, peer)
    own = [
        pltpu.make_async_copy(blocks[n], alls[n].at[mine], own_sem.at[n]) for n in range(arrays)
    ]
    for copy in own:
        copy.start()
    for a in line_peers:
        slot = index(a, place, core)
        arrived(slot)
        for b in row_peers:
            push(held(slot), slot, (line, b, core))
        for c in core_peers:
            push(held(slot), slot, (line, place, c))
    for a in [line] + line_peers:
        for b in row_peers:
            slot = index(a, b, core)
            arrived(slot)
            for c in core_peers:
                push(held(slot), slot, (line, place, c))
    for c in core_peers:
        for a in [line] + line_peers:
            for b in [place] + row_peers:
                arrived(index(a, b, c))
    for copy in own:
        copy.wait()
    for copy in sent:
        copy.wait_send()


def gather_blocks(blocks, collective_id):
    owners, cores = lax.axis_size("owner"), lax.axis_size("dp")
    along = 2 if owners < 16 else 8
    lines = owners // along
    arrays = len(blocks)
    copies = lines + along + cores - 3
    copies += (lines - 1) * (along + cores - 2) + lines * (along - 1) * (cores - 1)
    return pl.pallas_call(
        functools.partial(gather_kernel, lines, along, arrays),
        in_specs=[pl.BlockSpec(memory_space=pl.ANY)] * arrays,
        out_specs=[pl.BlockSpec(memory_space=pl.ANY)] * arrays,
        out_shape=[
            jax.ShapeDtypeStruct((owners * cores,) + block.shape, block.dtype) for block in blocks
        ],
        scratch_shapes=[
            pltpu.SemaphoreType.DMA((arrays * copies,)),
            pltpu.SemaphoreType.DMA((arrays, owners * cores)),
            pltpu.SemaphoreType.DMA((arrays,)),
        ],
        compiler_params=pltpu.CompilerParams(
            collective_id=collective_id, has_side_effects=True
        ),
        cost_estimate=pl.CostEstimate(
            flops=0,
            bytes_accessed=4 * owners * cores * sum(block.size for block in blocks),
            transcendentals=0,
        ),
    )(*blocks)


def exchange_blocks(block, later):
    owners, cores = lax.axis_size("owner"), lax.axis_size("dp")
    count = owners * cores
    place = jnp.arange(count, dtype=jnp.int32)
    if count > 32:
        return lax.all_gather(block, BOTH, axis=0), place, later
    quad = 4
    far = count // quad
    pieces = [block]
    for s in range(1, quad):
        pairs = [(i, i // quad * quad + (i + s) % quad) for i in range(count)]
        pieces.append(lax.ppermute(block, BOTH, pairs))
    near, later = lax.optimization_barrier((jnp.stack(pieces), later))
    groups = [near]
    for s in range(1, far):
        pairs = [(i, (i + quad * s) % count) for i in range(count)]
        groups.append(lax.ppermute(near, BOTH, pairs))
    me = lax.axis_index("owner") * cores + lax.axis_index("dp")
    order = (me // quad - place // quad + far) % far * quad + (me - place + count) % quad
    return jnp.concatenate(groups, axis=0), order, later


def score_kernel(rollouts, per, order_ref, *refs):
    out_refs = refs[:per]
    sel_out_ref, eig_ref, masked_ref, sel_in_ref, acc_ref = refs[per:]

    @pl.when(pl.program_id(0) == 0)
    def _():
        acc_ref[...] = jnp.zeros_like(acc_ref)

    rows = eig_ref.shape[0]
    wide = sel_in_ref.shape[1]
    damped = eig_ref[...].astype(jnp.float32) + DAMPING
    rough = pl.reciprocal(damped, approx=True)
    inv = rough * (2.0 - damped * rough)
    tokens_t = jnp.concatenate([ref[0].T for ref in out_refs], axis=0)
    sel_out = sel_out_ref[...].astype(jnp.float32)
    for e in range(rollouts):
        outer = jnp.dot(tokens_t, masked_ref[e], preferred_element_type=jnp.float32)
        scaled = (outer * inv).astype(jnp.bfloat16)
        turned = jnp.dot(scaled, sel_in_ref[...], preferred_element_type=jnp.float32)
        acc_ref[e] += jnp.sum((turned * sel_out).reshape(rows // 8, 8, wide), axis=0)


def plane_scores(order, rot_out, sel_out_t, eigvals, masked_in, sel_in_t):
    total, columns = eigvals.shape
    rollouts, tokens, _ = masked_in.shape
    wide = sel_in_t.shape[1]
    block = rot_out.shape[2]
    per = max(1, 1024 // block)
    rows = per * block

    def rotated(n):
        return pl.BlockSpec((1, tokens, block), lambda i, order: (order[i * per + n], 0, 0))

    return pl.pallas_call(
        functools.partial(score_kernel, rollouts, per),
        grid_spec=pltpu.PrefetchScalarGridSpec(
            num_scalar_prefetch=1,
            grid=(total // rows,),
            in_specs=[rotated(n) for n in range(per)]
            + [
                pl.BlockSpec((rows, wide), lambda i, order: (i, 0)),
                pl.BlockSpec((rows, columns), lambda i, order: (i, 0)),
                pl.BlockSpec((rollouts, tokens, columns), lambda i, order: (0, 0, 0)),
                pl.BlockSpec((columns, wide), lambda i, order: (0, 0)),
            ],
            out_specs=pl.BlockSpec((rollouts, 8, wide), lambda i, order: (0, 0, 0)),
        ),
        out_shape=jax.ShapeDtypeStruct((rollouts, 8, wide), jnp.float32),
        compiler_params=pltpu.CompilerParams(vmem_limit_bytes=56 * 1024 * 1024),
        cost_estimate=pl.CostEstimate(
            flops=2 * rollouts * total * columns * (wide + 256),
            bytes_accessed=2 * total * (columns + wide),
            transcendentals=total * columns,
        ),
    )(order, *[rot_out] * per, sel_out_t, eigvals, masked_in, sel_in_t)


def on_device(
    activations,
    out_grads,
    lengths,
    rollout_ids,
    basis_in,
    basis_out,
    eigvals,
    query_out,
    query_in,
    query_ids,
):
    queries = query_ids.shape[0]
    bank, rank, _ = query_out.shape
    slots = activations.shape[1]
    owners = lax.axis_size("owner")
    replicas = lax.axis_size("dp")
    per_replica = lengths.shape[1]
    rollouts = rollout_ids.shape[0]
    tokens = owners * replicas * slots
    picker = (query_ids[:, None] == jnp.arange(bank, dtype=jnp.int32)[None, :]).astype(jnp.bfloat16)

    wide_in, wide_out = activations.shape[2], out_grads.shape[2]
    sel_out_t = jnp.einsum(
        "qb,brj->jqr", picker, query_out, preferred_element_type=jnp.float32
    ).astype(jnp.bfloat16)
    sel_out_t = lax.all_gather(sel_out_t.reshape(-1, queries * rank), BOTH, axis=0, tiled=True)
    sel_in_t = jnp.einsum(
        "qb,brk->kqr", picker, query_in, preferred_element_type=jnp.float32
    ).astype(jnp.bfloat16)
    sel_in_t = sel_in_t.reshape(-1, queries * rank)

    acts, grads = gather_blocks([activations.reshape(-1, 128), out_grads.reshape(-1, 128)], 0)
    acts = acts.reshape(tokens, wide_in)
    grads = grads.reshape(tokens, wide_out)
    block_out = jnp.dot(grads, basis_out, preferred_element_type=jnp.float32).astype(jnp.bfloat16)
    rot_out, order, acts = exchange_blocks(block_out, acts)
    rot_in = jnp.dot(acts, basis_in, preferred_element_type=jnp.float32).astype(jnp.bfloat16)

    token = jnp.arange(tokens, dtype=jnp.int32)
    place = (token // (replicas * slots)) * slots + token % slots
    replica = (token // slots) % replicas
    ends = jnp.cumsum(lengths, axis=1)
    starts = ends - lengths
    member = (
        (jnp.arange(replicas, dtype=jnp.int32)[:, None, None] == replica[None, None, :])
        & (place[None, None, :] >= starts[:, :, None])
        & (place[None, None, :] < ends[:, :, None])
    ).reshape(rollouts, tokens)
    masked_in = jnp.where(member[:, :, None], rot_in[None], jnp.zeros((), rot_in.dtype))

    acc = plane_scores(order, rot_out, sel_out_t, eigvals, masked_in, sel_in_t)
    scores = jnp.sum(acc.reshape(rollouts, 8, queries, rank), axis=(1, 3))
    shares = gather_blocks([jnp.pad(scores, ((0, 0), (0, -queries % 128)))], 1)[0]
    scores = jnp.sum(shares, axis=0)[:, :queries]
    placing = (rollout_ids[:, None] == jnp.arange(rollouts, dtype=jnp.int32)[None, :]).astype(
        jnp.float32
    )
    return jnp.sum(placing[:, :, None] * scores[:, None, :], axis=0)


def solution(mesh):
    return jax.shard_map(
        on_device,
        mesh=mesh,
        in_specs=(
            P(("groups", "dp"), "owner", None),
            P(("groups", "dp"), "owner", None),
            P("groups", None),
            P("groups"),
            P(None, BOTH),
            P(None, BOTH),
            P(None, BOTH),
            P(None, None, BOTH),
            P(None, None, BOTH),
            P("groups"),
        ),
        out_specs=P("groups", None),
        check_vma=False,
    )
```
